32 devices in a mesh: mp: 4 (over y, core), replica: 8 (over z, x).
Axes of the slice: x: 2, y: 2, z: 4, core: 2. Of those that a mesh axis runs over, the one named last changes fastest.
Arguments:
- weight: float32 [2560, 5120], P('mp'), may hold values from -6 to 6
- first_moment: bfloat16 [8, 2560, 5120], P('replica', 'mp'), may hold values from -0.0011978149 to 0.0011978149
- second_moment: bfloat16 [8, 2560, 5120], P('replica', 'mp'), may hold values from 9.95351e-09 to 9.983778e-07
- outer_momentum: float32 [2560, 5120], P(('mp', 'replica')), may hold values from -0.3 to 0.3
- act_table: bfloat16 [2048, 5120], P(None, 'mp'), may hold values from -6 to 6
- token_ids: int32 [8, 2, 512], P('replica'), may hold values from 0 to 2047
- targets: bfloat16 [8, 2, 512, 2560], P('replica', None, None, 'mp'), may hold values from -6 to 6
Outputs:
- new_weight: float32 [2560, 5120], P('mp')
- momentum: float32 [2560, 5120], P(('mp', 'replica'))
The draws below stay inside these ranges and needn't reach their ends.
All inputs are finite; a program needn't handle non-finite values. Where the reference program divides by a largest or mean magnitude, that divisor is 1e-20 or more.
Results may differ from the reference program's by a relative error of at most 0.002.
Values may be sent and summed in bfloat16 or wider, within the bound.
A program may use at most 128 MiB of HBM per device.

```python
import math
import jax
import jax.numpy as jnp
from jax import lax

D_IN = 5120
D_OUT = 2560
TOK = 512
STEPS = 2
TABLE = 2048
BLOCK = 128
PRIOR_STEPS = 3
REPLICAS = 8


def set_ends(array, rng, least, largest):
    place = [jax.random.randint(jax.random.fold_in(rng, axis), (), 0, length) for axis, length in enumerate(array.shape)]
    widest = array.shape.index(max(array.shape))
    beside = place[:widest] + [(place[widest] + 1) % array.shape[widest]] + place[widest + 1:]
    return array.at[tuple(place)].set(least).at[tuple(beside)].set(largest)


def levels(own_key, shape, shards, smallest, top_value):
    loudness = 1.0
    for dim, shards_of in shards:
        draws = jax.random.uniform(jax.random.fold_in(jax.random.fold_in(own_key, 6), dim), (shards_of,), jnp.float32, smallest / len(shards), top_value / len(shards))
        loudness = loudness * jnp.repeat(jnp.exp(draws), shape[dim] // shards_of).reshape((-1,) + (1,) * (len(shape) - 1 - dim))
    return loudness


def bell_draw(stream_key, dims, spread, reach, split=(), kind=jnp.bfloat16):
    gain = levels(stream_key, dims, split, -0.22, 0.18) if split else 1.0
    drawn = jax.random.normal(stream_key, dims, jnp.float32) * spread * gain
    return jnp.minimum(jnp.maximum(drawn, -reach), reach).astype(kind)


def setup_inputs(seed: int = 0) -> dict:
    seeds = jax.random.split(jax.random.key(seed), 8)
    weight = bell_draw(seeds[0], (D_OUT, D_IN), 1.0, 6.0, ((0, 4),), jnp.float32)
    first_moment = bell_draw(seeds[1], (REPLICAS, D_OUT, D_IN), 0.0002, 0.0011978149, ((0, 8), (1, 4)))
    second_moment = jnp.clip(jnp.exp(math.log(9.98377799987793e-07) - 4.6082065 * jax.random.uniform(seeds[2], (REPLICAS, D_OUT, D_IN), jnp.float32) ** levels(seeds[2], (REPLICAS, D_OUT, D_IN), ((0, 8), (1, 4)), -0.2, 0.2)), 9.953510016202927e-09, 9.98377799987793e-07).astype(jnp.bfloat16)
    outer_momentum = bell_draw(seeds[3], (D_OUT, D_IN), 0.05, 0.3, ((0, 32),), jnp.float32)
    act_table = bell_draw(seeds[4], (TABLE, D_IN), 1.0, 6.0, ((1, 4),))
    token_ids = set_ends(jax.random.randint(seeds[5], (REPLICAS, STEPS, TOK), 0, TABLE), jax.random.fold_in(seeds[5], 1), 0, TABLE - 1).astype(jnp.int32)
    targets = bell_draw(seeds[6], (REPLICAS, STEPS, TOK, D_OUT), 1.0, 6.0, ((0, 8), (3, 4)))
    return {"weight": weight, "first_moment": first_moment, "second_moment": second_moment, "outer_momentum": outer_momentum, "act_table": act_table, "token_ids": token_ids, "targets": targets}


beta_first = 0.9
beta_second = 0.95
adam_epsilon = 1e-08
inner_rate = 0.1
weight_decay = 0.1
outer_mu = 0.9
outer_rate = 0.7
scale_epsilon = 1e-06

def encode(values):
    row_count = values.shape[0]
    blocks = values.reshape(row_count, -1, BLOCK)
    scales = (lax.optimization_barrier(jnp.max(jnp.abs(blocks), axis=2)) + scale_epsilon).astype(jnp.bfloat16)
    code_values = (blocks / scales.astype(jnp.float32)[:, :, None]).astype(jnp.bfloat16)
    return (code_values.reshape(row_count, -1), scales)

def decode(code_values, scales):
    row_count = code_values.shape[0]
    blocks = code_values.astype(jnp.float32).reshape(row_count, scales.shape[1], -1)
    return (blocks * scales.astype(jnp.float32)[:, :, None]).reshape(row_count, -1)

def inner_steps(weight, first, second, table_rows, wanted_all, act_table):
    factor = D_IN ** (-0.5)
    current = weight
    moment_one = first.astype(jnp.float32)
    moment_two = second.astype(jnp.float32)
    for inner_step in range(STEPS):
        inputs = jnp.take(act_table, table_rows[inner_step], axis=0)
        weight_half = current.astype(jnp.bfloat16)
        output = jnp.dot(inputs, weight_half.T, preferred_element_type=jnp.float32) * factor
        signal = (output - wanted_all[inner_step].astype(jnp.float32)).astype(jnp.bfloat16)
        gradient = jnp.dot(signal.T, inputs, preferred_element_type=jnp.float32) * (factor / TOK)
        step_count = PRIOR_STEPS + inner_step + 1
        moment_one = beta_first * moment_one + (1.0 - beta_first) * gradient
        moment_two = beta_second * moment_two + (1.0 - beta_second) * gradient * gradient
        update = moment_one / (1.0 - beta_first ** step_count) / (jnp.sqrt(moment_two / (1.0 - beta_second ** step_count)) + adam_epsilon)
        current = current - inner_rate * (update + weight_decay * current)
    return weight - current

def reference(weight, first_moment, second_moment, outer_momentum, act_table, token_ids, targets):

    def add_replica(running, replica_index):
        delta = inner_steps(weight, first_moment[replica_index], second_moment[replica_index], token_ids[replica_index], targets[replica_index], act_table)
        code_values, scales = encode(delta)
        return (running + decode(code_values, scales), None)
    summed, _ = lax.scan(add_replica, jnp.zeros(weight.shape, jnp.float32), jnp.arange(REPLICAS, dtype=jnp.int32))
    average = summed / REPLICAS
    momentum = outer_mu * outer_momentum + average
    outer_update = average + outer_mu * momentum
    update_codes, update_scales = encode(outer_update)
    new_weight = weight - outer_rate * decode(update_codes, update_scales)
    return (new_weight, momentum)
```

```python
import functools

import jax
import jax.numpy as jnp
from jax import lax
from jax.experimental import pallas as pl
from jax.experimental.pallas import tpu as pltpu
from jax.sharding import PartitionSpec as P

STEPS = 2
BLOCK = 128
PRIOR_STEPS = 3


beta_first = 0.9
beta_second = 0.95
adam_epsilon = 1e-08
inner_rate = 0.1
weight_decay = 0.1
outer_mu = 0.9
outer_rate = 0.7
scale_epsilon = 1e-06


def encode(values):
    row_count = values.shape[0]
    blocks = values.reshape(row_count, -1, BLOCK)
    scales = (jnp.max(jnp.abs(blocks), axis=2) + scale_epsilon).astype(jnp.bfloat16)
    code_values = (blocks / scales.astype(jnp.float32)[:, :, None]).astype(jnp.bfloat16)
    return (code_values.reshape(row_count, -1), scales)


def decode(code_values, scales):
    row_count = code_values.shape[0]
    blocks = code_values.astype(jnp.float32).reshape(row_count, scales.shape[1], -1)
    return (blocks * scales.astype(jnp.float32)[:, :, None]).reshape(row_count, -1)


def shards_plain(weight, first_moment, second_moment, outer_momentum, act_table, token_ids, targets):
    row_count, width = weight.shape
    tokens_step = token_ids.shape[2]
    factor = width ** (-0.5)
    current = weight
    moment_one = first_moment[0].astype(jnp.float32)
    moment_two = second_moment[0].astype(jnp.float32)
    for inner_step in range(STEPS):
        local_inputs = jnp.take(act_table, token_ids[0, inner_step], axis=0)
        weight_half = current.astype(jnp.bfloat16)
        wanted = targets[0, inner_step].astype(jnp.float32)
        inputs = lax.all_gather(local_inputs, "mp", axis=1, tiled=True)
        output = (
            lax.dot_general(
                inputs, weight_half, (((1,), (1,)), ((), ())), preferred_element_type=jnp.float32
            )
            * factor
        )
        signal = (output - wanted).astype(jnp.bfloat16)
        gradient = lax.dot_general(
            signal, inputs, (((0,), (0,)), ((), ())), preferred_element_type=jnp.float32
        ) * (factor / tokens_step)
        step_count = PRIOR_STEPS + inner_step + 1
        moment_one = beta_first * moment_one + (1.0 - beta_first) * gradient
        moment_two = beta_second * moment_two + (1.0 - beta_second) * gradient * gradient
        update = (
            moment_one
            / (1.0 - beta_first**step_count)
            / (jnp.sqrt(moment_two / (1.0 - beta_second**step_count)) + adam_epsilon)
        )
        current = current - inner_rate * (update + weight_decay * current)
    delta = weight - current
    code_values, scales = encode(delta)
    replicas = lax.axis_size("replica")
    fragment = row_count // replicas
    blocks_row = scales.shape[1]
    got_codes, got_scales = (
        lax.all_to_all(
            code_values.reshape(replicas, fragment, width),
            "replica",
            split_axis=0,
            concat_axis=0,
            tiled=True,
        ),
        lax.all_to_all(
            scales.reshape(replicas, fragment, blocks_row),
            "replica",
            split_axis=0,
            concat_axis=0,
            tiled=True,
        ),
    )
    decoded = decode(
        got_codes.reshape(replicas * fragment, width),
        got_scales.reshape(replicas * fragment, blocks_row),
    )
    summed = jnp.sum(decoded.reshape(replicas, fragment, width), axis=0)
    average = summed / replicas
    momentum = outer_mu * outer_momentum + average
    outer_update = average + outer_mu * momentum
    update_codes, update_scales = encode(outer_update)
    all_codes, all_scales = (
        lax.all_gather(update_codes, "replica", axis=0, tiled=True),
        lax.all_gather(update_scales, "replica", axis=0, tiled=True),
    )
    new_weight = weight - outer_rate * decode(all_codes, all_scales)
    return (new_weight, momentum)


MESH = pl.DeviceIdType.MESH
TILE = 16


def adam(current, moment_one, moment_two, gradient, unit, step_count):
    one = beta_first * moment_one + ((1.0 - beta_first) * unit) * gradient
    two = beta_second * moment_two + ((1.0 - beta_second) * unit * unit) * (gradient * gradient)
    spread = two * (1.0 / (1.0 - beta_second**step_count))
    bottom = spread * lax.rsqrt(spread) + adam_epsilon
    update = (one * (inner_rate / (1.0 - beta_first**step_count))) / bottom
    return (1.0 - inner_rate * weight_decay) * current - update, one, two


def inner_kernel(
    chunks, factor, unit, x1, x2, w, m, v, t1, t2, codes, scales, acc, s1, s2, g1, g2, half, all_scales
):
    phase, chunk = pl.program_id(0), pl.program_id(1)
    row_count, wide = w.shape
    rows_of = lambda i: pl.ds(pl.multiple_of(i * TILE, TILE), TILE)

    def add_output(weights, inputs, wanted, signal):
        part = lax.dot_general(
            weights, inputs, (((1,), (1,)), ((), ())), preferred_element_type=jnp.float32
        )

        @pl.when(chunk == 0)
        def _():
            acc[...] = part

        @pl.when(chunk > 0)
        def _():
            acc[...] += part

        @pl.when(chunk == chunks - 1)
        def _():
            signal[...] = (acc[...] * factor - wanted[...].astype(jnp.float32)).astype(jnp.bfloat16)

    def first_step(rows):
        return adam(
            w[rows, :],
            m[rows, :].astype(jnp.float32),
            v[rows, :].astype(jnp.float32),
            g1[chunk, rows, :],
            unit,
            PRIOR_STEPS + 1,
        )

    @pl.when(phase == 0)
    def _():
        add_output(w[...].astype(jnp.bfloat16), x1[...], t1, s1)

    @pl.when(phase == 1)
    def _():
        g1[chunk] = jnp.dot(s1[...], x1[...], preferred_element_type=jnp.float32)

        def body(i, carry):
            half[rows_of(i), :] = first_step(rows_of(i))[0].astype(jnp.bfloat16)
            return carry

        lax.fori_loop(0, row_count // TILE, body, 0, unroll=2)
        add_output(half[...], x2[...], t2, s2)

    @pl.when(phase == 2)
    def _():
        g2[...] = jnp.dot(s2[...], x2[...], preferred_element_type=jnp.float32)
        lane = lax.broadcasted_iota(jnp.int32, (TILE, BLOCK), 1)

        @pl.when(chunk == 0)
        def _():
            all_scales[...] = jnp.zeros_like(all_scales)

        def body(i, carry):
            rows = rows_of(i)
            current, one, two = first_step(rows)
            current, _, _ = adam(current, one, two, g2[rows, :], unit, PRIOR_STEPS + 2)
            delta = w[rows, :] - current
            kept = all_scales[rows, :]
            for block in range(wide // BLOCK):
                values = delta[:, block * BLOCK : (block + 1) * BLOCK]
                largest = jnp.max(jnp.abs(values), axis=1, keepdims=True)
                scale = (largest + scale_epsilon).astype(jnp.bfloat16).astype(jnp.float32)
                codes[rows, block * BLOCK : (block + 1) * BLOCK] = (values / scale).astype(jnp.bfloat16)
                kept = jnp.where(lane == chunk * (wide // BLOCK) + block, scale, kept)
            all_scales[rows, :] = kept
            return carry

        lax.fori_loop(0, row_count // TILE, body, 0, unroll=2)

        @pl.when(chunk == chunks - 1)
        def _():
            scales[...] = all_scales[...].astype(jnp.bfloat16)


def inner_steps(inputs, weight, first, second, wanted):
    row_count, width = weight.shape
    tokens = wanted.shape[2]
    wide = 512 if width % 512 == 0 else BLOCK
    chunks = width // wide
    factor = width ** (-0.5)
    later = lambda phase, chunk: chunk * jnp.minimum(phase, 1)
    columns = lambda phase, chunk: (0, chunk)
    whole = lambda phase, chunk: (0, 0)
    return pl.pallas_call(
        functools.partial(inner_kernel, chunks, factor, factor / tokens),
        grid=(3, chunks),
        out_shape=(
            jax.ShapeDtypeStruct((row_count, width), jnp.bfloat16),
            jax.ShapeDtypeStruct((row_count, BLOCK), jnp.bfloat16),
        ),
        in_specs=[
            pl.BlockSpec((tokens, wide), lambda phase, chunk: (0, jnp.where(phase < 2, chunk, chunks - 1))),
            pl.BlockSpec((tokens, wide), lambda phase, chunk: (1, later(phase, chunk))),
            pl.BlockSpec((row_count, wide), columns),
            pl.BlockSpec((row_count, wide), lambda phase, chunk: (0, later(phase, chunk))),
            pl.BlockSpec((row_count, wide), lambda phase, chunk: (0, later(phase, chunk))),
            pl.BlockSpec((row_count, tokens), whole),
            pl.BlockSpec((row_count, tokens), whole),
        ],
        out_specs=(
            pl.BlockSpec((row_count, wide), lambda phase, chunk: (0, chunk * (phase // 2))),
            pl.BlockSpec((row_count, BLOCK), whole),
        ),
        scratch_shapes=[
            pltpu.VMEM((row_count, tokens), jnp.float32),
            pltpu.VMEM((row_count, tokens), jnp.bfloat16),
            pltpu.VMEM((row_count, tokens), jnp.bfloat16),
            pltpu.VMEM((chunks, row_count, wide), jnp.float32),
            pltpu.VMEM((row_count, wide), jnp.float32),
            pltpu.VMEM((row_count, wide), jnp.bfloat16),
            pltpu.VMEM((row_count, BLOCK), jnp.float32),
        ],
        compiler_params=pltpu.CompilerParams(vmem_limit_bytes=48 * 2**20),
        cost_estimate=pl.CostEstimate(
            flops=8 * row_count * width * tokens, bytes_accessed=30 * row_count * width, transcendentals=0
        ),
    )(inputs, inputs, weight, first, second, wanted[0], wanted[1])


def flipped(place, bits):
    bit = 1
    while bit <= bits:
        if bits & bit:
            place = place + bit * (1 - 2 * lax.rem(place // bit, 2))
        bit *= 2
    return place


PARTS = 2


def exchange_kernel(
    replicas, codes, scales, outer, momentum, update, got_codes, got_scales, pair_out, pair_in, own,
    code_send, code_recv, scale_send, scale_recv, pair_send, pair_recv,
):
    groups = replicas // 2
    me = lax.axis_index("replica")
    group, side = me // 2, lax.rem(me, 2)
    partner = 2 * group + 1 - side
    fragment, width = outer.shape
    wide = width // PARTS

    barrier = pltpu.get_barrier_semaphore()
    pl.semaphore_signal(barrier, inc=1, device_id={"replica": partner}, device_id_type=MESH)
    for turn in range(1, groups):
        pl.semaphore_signal(
            barrier, inc=1, device_id={"replica": 2 * flipped(group, turn) + side}, device_id_type=MESH
        )
    pl.semaphore_wait(barrier, groups)

    order = [(turn, part) for turn in range(groups - 1, -1, -1) for part in range(PARTS)]

    def code_copy(i):
        turn, part = order[i]
        columns = pl.ds(part * wide, wide)
        return pltpu.make_async_remote_copy(
            src_ref=codes.at[2 * flipped(group, turn) + 1 - side, :, columns],
            dst_ref=got_codes.at[turn, :, columns],
            send_sem=code_send.at[i],
            recv_sem=code_recv.at[i],
            device_id={"replica": partner},
            device_id_type=MESH,
        )

    def scale_copy(turn):
        return pltpu.make_async_remote_copy(
            src_ref=scales.at[2 * flipped(group, turn) + 1 - side],
            dst_ref=got_scales.at[turn],
            send_sem=scale_send.at[turn],
            recv_sem=scale_recv.at[turn],
            device_id={"replica": partner},
            device_id_type=MESH,
        )

    def pair_copy(i):
        turn, part = order[i]
        columns = pl.ds(part * wide, wide)
        return pltpu.make_async_remote_copy(
            src_ref=pair_out.at[turn - 1, :, columns],
            dst_ref=pair_in.at[turn - 1, :, columns],
            send_sem=pair_send.at[i],
            recv_sem=pair_recv.at[i],
            device_id={"replica": 2 * flipped(group, turn) + side},
            device_id_type=MESH,
        )

    for turn in range(groups):
        scale_copy(turn).start()
    code_copy(0).start()
    code_copy(1).start()
    for i, (turn, part) in enumerate(order):
        if part == 0:
            scale_copy(turn).wait()
        code_copy(i).wait()
        if i + 2 < len(order):
            code_copy(i + 2).start()
        mine = 2 * flipped(group, turn) + side

        def body(step, carry):
            rows = pl.ds(pl.multiple_of(step * TILE, TILE), TILE)
            my_scales = scales[mine, rows, :].astype(jnp.float32)
            their_scales = got_scales[turn, rows, :].astype(jnp.float32)
            for block in range(wide // BLOCK):
                at = part * (wide // BLOCK) + block
                columns = slice(at * BLOCK, (at + 1) * BLOCK)
                total = (
                    codes[mine, rows, columns].astype(jnp.float32) * my_scales[:, at : at + 1]
                    + got_codes[turn, rows, columns].astype(jnp.float32) * their_scales[:, at : at + 1]
                )
                if turn:
                    pair_out[turn - 1, rows, columns] = total.astype(jnp.bfloat16)
                else:
                    own[rows, columns] = total
            return carry

        lax.fori_loop(0, fragment // TILE, body, 0)
        if turn:
            pair_copy(i).start()
    for i, (turn, part) in enumerate(order):
        if turn:
            pair_copy(i).wait()

    def finish(step, carry):
        rows = pl.ds(pl.multiple_of(step * TILE, TILE), TILE)
        for at in range(width // (4 * BLOCK)):
            columns = slice(at * 4 * BLOCK, (at + 1) * 4 * BLOCK)
            total = own[rows, columns]
            for turn in range(1, groups):
                total = total + pair_in[turn - 1, rows, columns].astype(jnp.float32)
            average = total * (1.0 / replicas)
            moved = outer_mu * outer[rows, columns] + average
            momentum[rows, columns] = moved
            update[rows, columns] = (average + outer_mu * moved).astype(jnp.bfloat16)
        return carry

    lax.fori_loop(0, fragment // TILE, finish, 0)


def exchange(codes, scales, outer_momentum, replicas):
    fragment, width = outer_momentum.shape
    groups = replicas // 2
    dma = pltpu.SemaphoreType.DMA
    vmem = pl.BlockSpec(memory_space=pltpu.VMEM)
    return pl.pallas_call(
        functools.partial(exchange_kernel, replicas),
        out_shape=(
            jax.ShapeDtypeStruct((fragment, width), jnp.float32),
            jax.ShapeDtypeStruct((fragment, width), jnp.bfloat16),
        ),
        in_specs=[vmem] * 3,
        out_specs=(vmem, vmem),
        scratch_shapes=[
            pltpu.VMEM((groups, fragment, width), jnp.bfloat16),
            pltpu.VMEM((groups, fragment, BLOCK), jnp.bfloat16),
            pltpu.VMEM((groups - 1, fragment, width), jnp.bfloat16),
            pltpu.VMEM((groups - 1, fragment, width), jnp.bfloat16),
            pltpu.VMEM((fragment, width), jnp.float32),
            dma((groups * PARTS,)),
            dma((groups * PARTS,)),
            dma((groups,)),
            dma((groups,)),
            dma((groups * PARTS,)),
            dma((groups * PARTS,)),
        ],
        compiler_params=pltpu.CompilerParams(
            collective_id=0, has_side_effects=True, vmem_limit_bytes=40 * 2**20
        ),
    )(codes.reshape(replicas, fragment, width), scales.reshape(replicas, fragment, BLOCK), outer_momentum)


def shards(weight, first_moment, second_moment, outer_momentum, act_table, token_ids, targets):
    row_count, width = weight.shape
    replicas = lax.axis_size("replica")
    fragment = row_count // replicas
    whole_tiles = fragment % TILE == 0 and width % (4 * BLOCK * PARTS) == 0 and width // BLOCK <= BLOCK
    if not whole_tiles or replicas < 4 or replicas & (replicas - 1):
        return shards_plain(
            weight, first_moment, second_moment, outer_momentum, act_table, token_ids, targets
        )
    local = jnp.take(act_table, token_ids[0].reshape(-1), axis=0, mode="clip")
    wanted = jnp.swapaxes(targets[0], 1, 2)
    inputs = lax.all_gather(local, "mp", axis=1, tiled=True)
    codes, scales = inner_steps(inputs, weight, first_moment[0], second_moment[0], wanted)
    momentum, update = exchange(codes, scales, outer_momentum, replicas)
    update = lax.all_gather(update, "replica", axis=0, tiled=True)
    return (weight - outer_rate * update.astype(jnp.float32), momentum)


def solution(mesh):
    in_specs = (
        P("mp", None),
        P("replica", "mp", None),
        P("replica", "mp", None),
        P(("mp", "replica"), None),
        P(None, "mp"),
        P("replica", None, None),
        P("replica", None, None, "mp"),
    )
    out_specs = (P("mp", None), P(("mp", "replica"), None))
    return jax.shard_map(shards, mesh=mesh, in_specs=in_specs, out_specs=out_specs, check_vma=False)
```

```python
import functools

import jax
import jax.numpy as jnp
from jax import lax
from jax.experimental import pallas as pl
from jax.experimental.pallas import tpu as pltpu
from jax.sharding import PartitionSpec as P

STEPS = 2
BLOCK = 128
PRIOR_STEPS = 3


beta_first = 0.9
beta_second = 0.95
adam_epsilon = 1e-08
inner_rate = 0.1
weight_decay = 0.1
outer_mu = 0.9
outer_rate = 0.7
scale_epsilon = 1e-06


def encode(values):
    row_count = values.shape[0]
    blocks = values.reshape(row_count, -1, BLOCK)
    scales = (jnp.max(jnp.abs(blocks), axis=2) + scale_epsilon).astype(jnp.bfloat16)
    code_values = (blocks / scales.astype(jnp.float32)[:, :, None]).astype(jnp.bfloat16)
    return (code_values.reshape(row_count, -1), scales)


def decode(code_values, scales):
    row_count = code_values.shape[0]
    blocks = code_values.astype(jnp.float32).reshape(row_count, scales.shape[1], -1)
    return (blocks * scales.astype(jnp.float32)[:, :, None]).reshape(row_count, -1)


def shards_plain(weight, first_moment, second_moment, outer_momentum, act_table, token_ids, targets):
    row_count, width = weight.shape
    tokens_step = token_ids.shape[2]
    factor = width ** (-0.5)
    current = weight
    moment_one = first_moment[0].astype(jnp.float32)
    moment_two = second_moment[0].astype(jnp.float32)
    for inner_step in range(STEPS):
        local_inputs = jnp.take(act_table, token_ids[0, inner_step], axis=0)
        weight_half = current.astype(jnp.bfloat16)
        wanted = targets[0, inner_step].astype(jnp.float32)
        inputs = lax.all_gather(local_inputs, "mp", axis=1, tiled=True)
        output = (
            lax.dot_general(
                inputs, weight_half, (((1,), (1,)), ((), ())), preferred_element_type=jnp.float32
            )
            * factor
        )
        signal = (output - wanted).astype(jnp.bfloat16)
        gradient = lax.dot_general(
            signal, inputs, (((0,), (0,)), ((), ())), preferred_element_type=jnp.float32
        ) * (factor / tokens_step)
        step_count = PRIOR_STEPS + inner_step + 1
        moment_one = beta_first * moment_one + (1.0 - beta_first) * gradient
        moment_two = beta_second * moment_two + (1.0 - beta_second) * gradient * gradient
        update = (
            moment_one
            / (1.0 - beta_first**step_count)
            / (jnp.sqrt(moment_two / (1.0 - beta_second**step_count)) + adam_epsilon)
        )
        current = current - inner_rate * (update + weight_decay * current)
    delta = weight - current
    code_values, scales = encode(delta)
    replicas = lax.axis_size("replica")
    fragment = row_count // replicas
    blocks_row = scales.shape[1]
    got_codes, got_scales = (
        lax.all_to_all(
            code_values.reshape(replicas, fragment, width),
            "replica",
            split_axis=0,
            concat_axis=0,
            tiled=True,
        ),
        lax.all_to_all(
            scales.reshape(replicas, fragment, blocks_row),
            "replica",
            split_axis=0,
            concat_axis=0,
            tiled=True,
        ),
    )
    decoded = decode(
        got_codes.reshape(replicas * fragment, width),
        got_scales.reshape(replicas * fragment, blocks_row),
    )
    summed = jnp.sum(decoded.reshape(replicas, fragment, width), axis=0)
    average = summed / replicas
    momentum = outer_mu * outer_momentum + average
    outer_update = average + outer_mu * momentum
    update_codes, update_scales = encode(outer_update)
    all_codes, all_scales = (
        lax.all_gather(update_codes, "replica", axis=0, tiled=True),
        lax.all_gather(update_scales, "replica", axis=0, tiled=True),
    )
    new_weight = weight - outer_rate * decode(all_codes, all_scales)
    return (new_weight, momentum)


MESH = pl.DeviceIdType.MESH
TILE = 16


def adam(current, moment_one, moment_two, gradient, unit, step_count):
    one = beta_first * moment_one + ((1.0 - beta_first) * unit) * gradient
    two = beta_second * moment_two + ((1.0 - beta_second) * unit * unit) * (gradient * gradient)
    spread = two * (1.0 / (1.0 - beta_second**step_count))
    root = lax.rsqrt(spread)
    bottom = spread * root + adam_epsilon
    inverse = root * (2.0 - bottom * root)
    update = (one * (inner_rate / (1.0 - beta_first**step_count))) * inverse
    return (1.0 - inner_rate * weight_decay) * current - update, one, two


def rows_of(i):
    return pl.ds(pl.multiple_of(i * TILE, TILE), TILE)


def add_output(chunk, chunks, factor, weights, inputs, wanted, acc, signal):
    part = lax.dot_general(
        weights, inputs, (((1,), (1,)), ((), ())), preferred_element_type=jnp.float32
    )

    @pl.when(chunk == 0)
    def _():
        acc[...] = part

    @pl.when(chunk > 0)
    def _():
        acc[...] += part

    @pl.when(chunk == chunks - 1)
    def _():
        signal[...] = (acc[...] * factor - wanted[...].astype(jnp.float32)).astype(jnp.bfloat16)


def first_kernel(chunks, factor, unit, x, w, m, v, t, current, first, second, acc, signal, gradient):
    phase, chunk = pl.program_id(0), pl.program_id(1)
    row_count, wide = w.shape

    @pl.when(phase == 0)
    def _():
        add_output(chunk, chunks, factor, w[...].astype(jnp.bfloat16), x[...], t, acc, signal)

    @pl.when(phase == 1)
    def _():
        gradient[...] = jnp.dot(signal[...], x[...], preferred_element_type=jnp.float32)

        def body(i, carry):
            rows = rows_of(i)
            for start in range(0, wide, 4 * BLOCK):
                columns = slice(start, min(start + 4 * BLOCK, wide))
                current[rows, columns], first[rows, columns], second[rows, columns] = adam(
                    w[rows, columns],
                    m[rows, columns].astype(jnp.float32),
                    v[rows, columns].astype(jnp.float32),
                    gradient[rows, columns],
                    unit,
                    PRIOR_STEPS + 1,
                )
            return carry

        lax.fori_loop(0, row_count // TILE, body, 0)


def second_kernel(
    chunks, factor, unit, x, w, current, first, second, t, codes, scales, acc, signal, gradient, all_scales
):
    phase, chunk = pl.program_id(0), pl.program_id(1)
    row_count, wide = w.shape

    @pl.when(phase == 0)
    def _():
        add_output(chunk, chunks, factor, current[...].astype(jnp.bfloat16), x[...], t, acc, signal)

    @pl.when(phase == 1)
    def _():
        gradient[...] = jnp.dot(signal[...], x[...], preferred_element_type=jnp.float32)
        lane = lax.broadcasted_iota(jnp.int32, (TILE, BLOCK), 1)

        @pl.when(chunk == 0)
        def _():
            all_scales[...] = jnp.zeros_like(all_scales)

        def body(i, carry):
            rows = rows_of(i)
            kept = all_scales[rows, :]
            for block in range(wide // BLOCK):
                columns = slice(block * BLOCK, (block + 1) * BLOCK)
                after, _, _ = adam(
                    current[rows, columns],
                    first[rows, columns],
                    second[rows, columns],
                    gradient[rows, columns],
                    unit,
                    PRIOR_STEPS + 2,
                )
                values = w[rows, columns] - after
                largest = jnp.max(jnp.abs(values), axis=1, keepdims=True)
                scale = (largest + scale_epsilon).astype(jnp.bfloat16).astype(jnp.float32)
                codes[rows, columns] = (values / scale).astype(jnp.bfloat16)
                kept = jnp.where(lane == chunk * (wide // BLOCK) + block, scale, kept)
            all_scales[rows, :] = kept
            return carry

        lax.fori_loop(0, row_count // TILE, body, 0)

        @pl.when(chunk == chunks - 1)
        def _():
            scales[...] = all_scales[...].astype(jnp.bfloat16)


def first_step(inputs, weight, first, second, wanted):
    row_count, width = weight.shape
    tokens = inputs.shape[0]
    wide = next(size for size in (1024, 512, BLOCK) if width % size == 0)
    chunks = width // wide
    factor = width ** (-0.5)
    columns = lambda phase, chunk: (0, chunk)
    later = lambda phase, chunk: (0, chunk * phase)
    kept = jax.ShapeDtypeStruct((row_count, width), jnp.float32)
    return pl.pallas_call(
        functools.partial(first_kernel, chunks, factor, factor / tokens),
        grid=(2, chunks),
        out_shape=(kept, kept, kept),
        in_specs=[
            pl.BlockSpec((tokens, wide), columns),
            pl.BlockSpec((row_count, wide), columns),
            pl.BlockSpec((row_count, wide), later),
            pl.BlockSpec((row_count, wide), later),
            pl.BlockSpec((row_count, tokens), lambda phase, chunk: (0, 0)),
        ],
        out_specs=(pl.BlockSpec((row_count, wide), later),) * 3,
        scratch_shapes=[
            pltpu.VMEM((row_count, tokens), jnp.float32),
            pltpu.VMEM((row_count, tokens), jnp.bfloat16),
            pltpu.VMEM((row_count, wide), jnp.float32),
        ],
        compiler_params=pltpu.CompilerParams(vmem_limit_bytes=48 * 2**20),
        cost_estimate=pl.CostEstimate(
            flops=4 * row_count * width * tokens, bytes_accessed=24 * row_count * width, transcendentals=0
        ),
    )(inputs, weight, first, second, wanted)


def second_step(inputs, weight, current, first, second, wanted):
    row_count, width = weight.shape
    tokens = inputs.shape[0]
    wide = next(size for size in (1024, 512, BLOCK) if width % size == 0)
    chunks = width // wide
    factor = width ** (-0.5)
    columns = lambda phase, chunk: (0, chunk)
    later = lambda phase, chunk: (0, chunk * phase)
    whole = lambda phase, chunk: (0, 0)
    return pl.pallas_call(
        functools.partial(second_kernel, chunks, factor, factor / tokens),
        grid=(2, chunks),
        out_shape=(
            jax.ShapeDtypeStruct((row_count, width), jnp.bfloat16),
            jax.ShapeDtypeStruct((row_count, BLOCK), jnp.bfloat16),
        ),
        in_specs=[
            pl.BlockSpec((tokens, wide), columns),
            pl.BlockSpec((row_count, wide), later),
            pl.BlockSpec((row_count, wide), columns),
            pl.BlockSpec((row_count, wide), later),
            pl.BlockSpec((row_count, wide), later),
            pl.BlockSpec((row_count, tokens), whole),
        ],
        out_specs=(
            pl.BlockSpec((row_count, wide), later),
            pl.BlockSpec((row_count, BLOCK), whole),
        ),
        scratch_shapes=[
            pltpu.VMEM((row_count, tokens), jnp.float32),
            pltpu.VMEM((row_count, tokens), jnp.bfloat16),
            pltpu.VMEM((row_count, wide), jnp.float32),
            pltpu.VMEM((row_count, BLOCK), jnp.float32),
        ],
        compiler_params=pltpu.CompilerParams(vmem_limit_bytes=48 * 2**20),
        cost_estimate=pl.CostEstimate(
            flops=4 * row_count * width * tokens, bytes_accessed=22 * row_count * width, transcendentals=0
        ),
    )(inputs, weight, current, first, second, wanted)


def flipped(place, bits):
    bit = 1
    while bit <= bits:
        if bits & bit:
            place = place + bit * (1 - 2 * lax.rem(place // bit, 2))
        bit *= 2
    return place


PARTS = 4
AHEAD = 3


def exchange_kernel(
    replicas, codes, scales, outer, momentum, updates, got_codes, got_scales, pair_out, pair_in, own, update,
    code_send, code_recv, scale_send, scale_recv, pair_send, pair_recv,
    along_send, along_recv, across_send, across_recv, keep,
):
    groups = replicas // 2
    me = lax.axis_index("replica")
    group, side = me // 2, lax.rem(me, 2)
    partner = 2 * group + 1 - side
    fragment, width = outer.shape
    wide = width // PARTS

    barrier = pltpu.get_barrier_semaphore()
    pl.semaphore_signal(barrier, inc=1, device_id={"replica": partner}, device_id_type=MESH)
    for turn in range(1, groups):
        pl.semaphore_signal(
            barrier, inc=1, device_id={"replica": 2 * flipped(group, turn) + side}, device_id_type=MESH
        )
    pl.semaphore_wait(barrier, groups)

    order = [(turn, part) for turn in range(groups - 1, -1, -1) for part in range(PARTS)]

    def code_copy(i):
        turn, part = order[i]
        columns = pl.ds(part * wide, wide)
        return pltpu.make_async_remote_copy(
            src_ref=codes.at[2 * flipped(group, turn) + 1 - side, :, columns],
            dst_ref=got_codes.at[turn, :, columns],
            send_sem=code_send.at[i],
            recv_sem=code_recv.at[i],
            device_id={"replica": partner},
            device_id_type=MESH,
        )

    def scale_copy(turn):
        return pltpu.make_async_remote_copy(
            src_ref=scales.at[2 * flipped(group, turn) + 1 - side],
            dst_ref=got_scales.at[turn],
            send_sem=scale_send.at[turn],
            recv_sem=scale_recv.at[turn],
            device_id={"replica": partner},
            device_id_type=MESH,
        )

    def pair_copy(i):
        turn, part = order[i]
        columns = pl.ds(part * wide, wide)
        return pltpu.make_async_remote_copy(
            src_ref=pair_out.at[turn - 1, :, columns],
            dst_ref=pair_in.at[turn - 1, :, columns],
            send_sem=pair_send.at[i],
            recv_sem=pair_recv.at[i],
            device_id={"replica": 2 * flipped(group, turn) + side},
            device_id_type=MESH,
        )

    for turn in range(groups):
        scale_copy(turn).start()
    for i in range(AHEAD):
        code_copy(i).start()
    for i, (turn, part) in enumerate(order):
        if part == 0:
            scale_copy(turn).wait()
        code_copy(i).wait()
        if i + AHEAD < len(order):
            code_copy(i + AHEAD).start()
        mine = 2 * flipped(group, turn) + side

        def body(step, carry):
            rows = pl.ds(pl.multiple_of(step * TILE, TILE), TILE)
            my_scales = scales[mine, rows, :].astype(jnp.float32)
            their_scales = got_scales[turn, rows, :].astype(jnp.float32)
            for block in range(wide // BLOCK):
                at = part * (wide // BLOCK) + block
                columns = slice(at * BLOCK, (at + 1) * BLOCK)
                total = (
                    codes[mine, rows, columns].astype(jnp.float32) * my_scales[:, at : at + 1]
                    + got_codes[turn, rows, columns].astype(jnp.float32) * their_scales[:, at : at + 1]
                )
                if turn:
                    pair_out[turn - 1, rows, columns] = total.astype(jnp.bfloat16)
                else:
                    own[rows, columns] = total
            return carry

        lax.fori_loop(0, fragment // TILE, body, 0)
        if turn:
            pair_copy(i).start()
    hops = []
    bit = groups // 2
    while bit:
        hops += [(bit, held) for held in range(0, groups, 2 * bit)]
        bit //= 2

    def place_of(held, part):
        return updates.at[2 * flipped(group, held) + side, :, pl.ds(part * wide, wide)]

    def source_of(held, part):
        return update.at[:, pl.ds(part * wide, wide)] if held == 0 else place_of(held, part)

    def along_copy(hop, part):
        bit, held = hops[hop]
        return pltpu.make_async_remote_copy(
            src_ref=source_of(held, part),
            dst_ref=place_of(held, part),
            send_sem=along_send.at[hop * PARTS + part],
            recv_sem=along_recv.at[hop * PARTS + part],
            device_id={"replica": 2 * flipped(group, bit) + side},
            device_id_type=MESH,
        )

    def across_copy(held, part):
        return pltpu.make_async_remote_copy(
            src_ref=source_of(held, part),
            dst_ref=place_of(held, part),
            send_sem=across_send.at[held * PARTS + part],
            recv_sem=across_recv.at[held * PARTS + part],
            device_id={"replica": partner},
            device_id_type=MESH,
        )

    def send_on(held, part):
        for hop, (bit, taken) in enumerate(hops):
            if taken == held:
                along_copy(hop, part).start()
        across_copy(held, part).start()

    for part in range(PARTS):
        for i, (turn, which) in enumerate(order):
            if turn and which == part:
                pair_copy(i).wait()

        def finish(step, carry):
            rows = pl.ds(pl.multiple_of(step * TILE, TILE), TILE)
            for start in range(part * wide, (part + 1) * wide, 2 * BLOCK):
                columns = slice(start, start + 2 * BLOCK)
                total = own[rows, columns]
                for turn in range(1, groups):
                    total = total + pair_in[turn - 1, rows, columns].astype(jnp.float32)
                average = total * (1.0 / replicas)
                moved = outer_mu * outer[rows, columns] + average
                momentum[rows, columns] = moved
                update[rows, columns] = (average + outer_mu * moved).astype(jnp.bfloat16)
            return carry

        lax.fori_loop(0, fragment // TILE, finish, 0)
        send_on(0, part)
    own_copy = pltpu.make_async_copy(update, updates.at[me], keep)
    own_copy.start()
    for hop, (bit, held) in enumerate(hops):
        for part in range(PARTS):
            along_copy(hop, part).wait_recv()
            send_on(held + bit, part)
    own_copy.wait()
    for part in range(PARTS):
        for hop in range(len(hops)):
            along_copy(hop, part).wait_send()
        for held in range(groups):
            across_copy(held, part).wait()


def exchange(codes, scales, outer_momentum, replicas):
    fragment, width = outer_momentum.shape
    groups = replicas // 2
    dma = pltpu.SemaphoreType.DMA
    vmem = pl.BlockSpec(memory_space=pltpu.VMEM)
    return pl.pallas_call(
        functools.partial(exchange_kernel, replicas),
        out_shape=(
            jax.ShapeDtypeStruct((fragment, width), jnp.float32),
            jax.ShapeDtypeStruct((replicas, fragment, width), jnp.bfloat16),
        ),
        in_specs=[vmem] * 3,
        out_specs=(vmem, pl.BlockSpec(memory_space=pl.ANY)),
        scratch_shapes=[
            pltpu.VMEM((groups, fragment, width), jnp.bfloat16),
            pltpu.VMEM((groups, fragment, BLOCK), jnp.bfloat16),
            pltpu.VMEM((groups - 1, fragment, width), jnp.bfloat16),
            pltpu.VMEM((groups - 1, fragment, width), jnp.bfloat16),
            pltpu.VMEM((fragment, width), jnp.float32),
            pltpu.VMEM((fragment, width), jnp.bfloat16),
            dma((groups * PARTS,)),
            dma((groups * PARTS,)),
            dma((groups,)),
            dma((groups,)),
            dma((groups * PARTS,)),
            dma((groups * PARTS,)),
            dma(((groups - 1) * PARTS,)),
            dma(((groups - 1) * PARTS,)),
            dma((groups * PARTS,)),
            dma((groups * PARTS,)),
            dma,
        ],
        compiler_params=pltpu.CompilerParams(
            collective_id=0, has_side_effects=True, vmem_limit_bytes=40 * 2**20
        ),
    )(codes.reshape(replicas, fragment, width), scales.reshape(replicas, fragment, BLOCK), outer_momentum)


def shards(weight, first_moment, second_moment, outer_momentum, act_table, token_ids, targets):
    row_count, width = weight.shape
    replicas = lax.axis_size("replica")
    fragment = row_count // replicas
    whole_tiles = fragment % TILE == 0 and width % (2 * BLOCK * PARTS) == 0 and width // BLOCK <= BLOCK
    if not whole_tiles or replicas < 4 or replicas & (replicas - 1):
        return shards_plain(
            weight, first_moment, second_moment, outer_momentum, act_table, token_ids, targets
        )
    wanted = jnp.swapaxes(targets[0], 1, 2)
    inputs = [
        lax.all_gather(
            jnp.take(act_table, token_ids[0, step], axis=0, mode="clip"), "mp", axis=1, tiled=True
        )
        for step in range(STEPS)
    ]
    current, first, second = first_step(inputs[0], weight, first_moment[0], second_moment[0], wanted[0])
    codes, scales = second_step(inputs[1], weight, current, first, second, wanted[1])
    momentum, updates = exchange(codes, scales, outer_momentum, replicas)
    update = updates.reshape(row_count, width).astype(jnp.float32)
    return (weight - outer_rate * update, momentum)


def solution(mesh):
    in_specs = (
        P("mp", None),
        P("replica", "mp", None),
        P("replica", "mp", None),
        P(("mp", "replica"), None),
        P(None, "mp"),
        P("replica", None, None),
        P("replica", None, None, "mp"),
    )
    out_specs = (P("mp", None), P(("mp", "replica"), None))
    return jax.shard_map(shards, mesh=mesh, in_specs=in_specs, out_specs=out_specs, check_vma=False)
```

```python
import functools

import jax
import jax.numpy as jnp
from jax import lax
from jax.experimental import pallas as pl
from jax.experimental.pallas import tpu as pltpu
from jax.sharding import PartitionSpec as P

STEPS = 2
BLOCK = 128
PRIOR_STEPS = 3


beta_first = 0.9
beta_second = 0.95
adam_epsilon = 1e-08
inner_rate = 0.1
weight_decay = 0.1
outer_mu = 0.9
outer_rate = 0.7
scale_epsilon = 1e-06


def encode(values):
    row_count = values.shape[0]
    blocks = values.reshape(row_count, -1, BLOCK)
    scales = (jnp.max(jnp.abs(blocks), axis=2) + scale_epsilon).astype(jnp.bfloat16)
    code_values = (blocks / scales.astype(jnp.float32)[:, :, None]).astype(jnp.bfloat16)
    return (code_values.reshape(row_count, -1), scales)


def decode(code_values, scales):
    row_count = code_values.shape[0]
    blocks = code_values.astype(jnp.float32).reshape(row_count, scales.shape[1], -1)
    return (blocks * scales.astype(jnp.float32)[:, :, None]).reshape(row_count, -1)


def shards_plain(weight, first_moment, second_moment, outer_momentum, act_table, token_ids, targets):
    row_count, width = weight.shape
    tokens_step = token_ids.shape[2]
    factor = width ** (-0.5)
    current = weight
    moment_one = first_moment[0].astype(jnp.float32)
    moment_two = second_moment[0].astype(jnp.float32)
    for inner_step in range(STEPS):
        local_inputs = jnp.take(act_table, token_ids[0, inner_step], axis=0)
        weight_half = current.astype(jnp.bfloat16)
        wanted = targets[0, inner_step].astype(jnp.float32)
        inputs = lax.all_gather(local_inputs, "mp", axis=1, tiled=True)
        output = (
            lax.dot_general(
                inputs, weight_half, (((1,), (1,)), ((), ())), preferred_element_type=jnp.float32
            )
            * factor
        )
        signal = (output - wanted).astype(jnp.bfloat16)
        gradient = lax.dot_general(
            signal, inputs, (((0,), (0,)), ((), ())), preferred_element_type=jnp.float32
        ) * (factor / tokens_step)
        step_count = PRIOR_STEPS + inner_step + 1
        moment_one = beta_first * moment_one + (1.0 - beta_first) * gradient
        moment_two = beta_second * moment_two + (1.0 - beta_second) * gradient * gradient
        update = (
            moment_one
            / (1.0 - beta_first**step_count)
            / (jnp.sqrt(moment_two / (1.0 - beta_second**step_count)) + adam_epsilon)
        )
        current = current - inner_rate * (update + weight_decay * current)
    delta = weight - current
    code_values, scales = encode(delta)
    replicas = lax.axis_size("replica")
    fragment = row_count // replicas
    blocks_row = scales.shape[1]
    got_codes, got_scales = (
        lax.all_to_all(
            code_values.reshape(replicas, fragment, width),
            "replica",
            split_axis=0,
            concat_axis=0,
            tiled=True,
        ),
        lax.all_to_all(
            scales.reshape(replicas, fragment, blocks_row),
            "replica",
            split_axis=0,
            concat_axis=0,
            tiled=True,
        ),
    )
    decoded = decode(
        got_codes.reshape(replicas * fragment, width),
        got_scales.reshape(replicas * fragment, blocks_row),
    )
    summed = jnp.sum(decoded.reshape(replicas, fragment, width), axis=0)
    average = summed / replicas
    momentum = outer_mu * outer_momentum + average
    outer_update = average + outer_mu * momentum
    update_codes, update_scales = encode(outer_update)
    all_codes, all_scales = (
        lax.all_gather(update_codes, "replica", axis=0, tiled=True),
        lax.all_gather(update_scales, "replica", axis=0, tiled=True),
    )
    new_weight = weight - outer_rate * decode(all_codes, all_scales)
    return (new_weight, momentum)


MESH = pl.DeviceIdType.MESH
TILE = 16


def adam(current, moment_one, moment_two, gradient, unit, step_count):
    one = beta_first * moment_one + ((1.0 - beta_first) * unit) * gradient
    two = beta_second * moment_two + ((1.0 - beta_second) * unit * unit) * (gradient * gradient)
    spread = two * (1.0 / (1.0 - beta_second**step_count))
    root = lax.rsqrt(spread)
    bottom = spread * root + adam_epsilon
    inverse = root * (2.0 - bottom * root)
    update = (one * (inner_rate / (1.0 - beta_first**step_count))) * inverse
    return (1.0 - inner_rate * weight_decay) * current - update, one, two


def rows_of(i):
    return pl.ds(pl.multiple_of(i * TILE, TILE), TILE)


def add_output(chunk, chunks, factor, weights, inputs, wanted, acc, signal):
    part = lax.dot_general(
        weights, inputs, (((1,), (1,)), ((), ())), preferred_element_type=jnp.float32
    )

    @pl.when(chunk == 0)
    def _():
        acc[...] = part

    @pl.when(chunk > 0)
    def _():
        acc[...] += part

    @pl.when(chunk == chunks - 1)
    def _():
        signal[...] = (acc[...] * factor - wanted[...].astype(jnp.float32)).astype(jnp.bfloat16)


def keep_piece(chunk, pieces, kept):
    for place, piece in enumerate(pieces):

        @pl.when(chunk == place)
        def _():
            kept[place] = piece[...]


def first_kernel(chunks, factor, unit, places, *refs):
    pieces, (w, m, v, t, current, first, second, acc, signal, gradient, x) = refs[:chunks], refs[chunks:]
    phase, chunk = pl.program_id(0), pl.program_id(1)
    row_count, wide = w.shape

    @pl.when(phase == 0)
    def _():
        keep_piece(chunk, pieces, x)
        add_output(chunk, chunks, factor, w[...].astype(jnp.bfloat16), x[chunk], t, acc, signal)

    @pl.when(phase == 1)
    def _():
        gradient[...] = jnp.dot(signal[...], x[chunk], preferred_element_type=jnp.float32)

        def body(i, carry):
            rows = rows_of(i)
            for start in range(0, wide, 4 * BLOCK):
                columns = slice(start, min(start + 4 * BLOCK, wide))
                current[rows, columns], first[rows, columns], second[rows, columns] = adam(
                    w[rows, columns],
                    m[rows, columns].astype(jnp.float32),
                    v[rows, columns].astype(jnp.float32),
                    gradient[rows, columns],
                    unit,
                    PRIOR_STEPS + 1,
                )
            return carry

        lax.fori_loop(0, row_count // TILE, body, 0)


def second_kernel(chunks, factor, unit, places, *refs):
    pieces, refs = refs[:chunks], refs[chunks:]
    w, current, first, second, t, codes, scales, acc, signal, gradient, all_scales, x = refs
    phase, chunk = pl.program_id(0), pl.program_id(1)
    row_count, wide = w.shape

    @pl.when(phase == 0)
    def _():
        keep_piece(chunk, pieces, x)
        add_output(chunk, chunks, factor, current[...].astype(jnp.bfloat16), x[chunk], t, acc, signal)

    @pl.when(phase == 1)
    def _():
        gradient[...] = jnp.dot(signal[...], x[chunk], preferred_element_type=jnp.float32)
        lane = lax.broadcasted_iota(jnp.int32, (TILE, BLOCK), 1)

        @pl.when(chunk == 0)
        def _():
            all_scales[...] = jnp.zeros_like(all_scales)

        def body(i, carry):
            rows = rows_of(i)
            kept = all_scales[rows, :]
            for block in range(wide // BLOCK):
                columns = slice(block * BLOCK, (block + 1) * BLOCK)
                after, _, _ = adam(
                    current[rows, columns],
                    first[rows, columns],
                    second[rows, columns],
                    gradient[rows, columns],
                    unit,
                    PRIOR_STEPS + 2,
                )
                values = w[rows, columns] - after
                largest = jnp.max(jnp.abs(values), axis=1, keepdims=True)
                scale = (largest + scale_epsilon).astype(jnp.bfloat16).astype(jnp.float32)
                codes[rows, columns] = (values / scale).astype(jnp.bfloat16)
                kept = jnp.where(lane == places[chunk] * (wide // BLOCK) + block, scale, kept)
            all_scales[rows, :] = kept
            return carry

        lax.fori_loop(0, row_count // TILE, body, 0)

        @pl.when(chunk == chunks - 1)
        def _():
            scales[...] = all_scales[...].astype(jnp.bfloat16)


def first_step(places, pieces, weight, first, second, wanted):
    row_count, width = weight.shape
    tokens, wide = pieces[0].shape
    chunks = len(pieces)
    factor = width ** (-0.5)
    columns = lambda phase, chunk, places: (0, places[chunk])
    later = lambda phase, chunk, places: (0, places[chunk * phase])
    kept = jax.ShapeDtypeStruct((row_count, width), jnp.float32)
    whole = lambda phase, chunk, places: (0, 0)
    once = pl.Buffered(1)
    return pl.pallas_call(
        functools.partial(first_kernel, chunks, factor, factor / tokens),
        out_shape=(kept, kept, kept),
        grid_spec=pltpu.PrefetchScalarGridSpec(
            num_scalar_prefetch=1,
            grid=(2, chunks),
        in_specs=[pl.BlockSpec((tokens, wide), whole, pipeline_mode=once)] * chunks
        + [
            pl.BlockSpec((row_count, wide), columns),
            pl.BlockSpec((row_count, wide), later),
            pl.BlockSpec((row_count, wide), later),
            pl.BlockSpec((row_count, tokens), whole, pipeline_mode=once),
        ],
        out_specs=(pl.BlockSpec((row_count, wide), later),) * 3,
        scratch_shapes=[
            pltpu.VMEM((row_count, tokens), jnp.float32),
            pltpu.VMEM((row_count, tokens), jnp.bfloat16),
            pltpu.VMEM((row_count, wide), jnp.float32),
            pltpu.VMEM((chunks, tokens, wide), jnp.bfloat16),
        ],
        ),
        compiler_params=pltpu.CompilerParams(vmem_limit_bytes=56 * 2**20),
        cost_estimate=pl.CostEstimate(
            flops=4 * row_count * width * tokens, bytes_accessed=24 * row_count * width, transcendentals=0
        ),
    )(places, *pieces, weight, first, second, wanted)


def second_step(places, pieces, weight, current, first, second, wanted):
    row_count, width = weight.shape
    tokens, wide = pieces[0].shape
    chunks = len(pieces)
    factor = width ** (-0.5)
    columns = lambda phase, chunk, places: (0, places[chunk])
    later = lambda phase, chunk, places: (0, places[chunk * phase])
    whole = lambda phase, chunk, places: (0, 0)
    once = pl.Buffered(1)
    return pl.pallas_call(
        functools.partial(second_kernel, chunks, factor, factor / tokens),
        out_shape=(
            jax.ShapeDtypeStruct((row_count, width), jnp.bfloat16),
            jax.ShapeDtypeStruct((row_count, BLOCK), jnp.bfloat16),
        ),
        grid_spec=pltpu.PrefetchScalarGridSpec(
            num_scalar_prefetch=1,
            grid=(2, chunks),
        in_specs=[pl.BlockSpec((tokens, wide), whole, pipeline_mode=once)] * chunks
        + [
            pl.BlockSpec((row_count, wide), later),
            pl.BlockSpec((row_count, wide), columns),
            pl.BlockSpec((row_count, wide), later),
            pl.BlockSpec((row_count, wide), later),
            pl.BlockSpec((row_count, tokens), whole, pipeline_mode=once),
        ],
        out_specs=(
            pl.BlockSpec((row_count, wide), later),
            pl.BlockSpec((row_count, BLOCK), whole),
        ),
        scratch_shapes=[
            pltpu.VMEM((row_count, tokens), jnp.float32),
            pltpu.VMEM((row_count, tokens), jnp.bfloat16),
            pltpu.VMEM((row_count, wide), jnp.float32),
            pltpu.VMEM((row_count, BLOCK), jnp.float32),
            pltpu.VMEM((chunks, tokens, wide), jnp.bfloat16),
        ],
        ),
        compiler_params=pltpu.CompilerParams(vmem_limit_bytes=56 * 2**20),
        cost_estimate=pl.CostEstimate(
            flops=4 * row_count * width * tokens, bytes_accessed=22 * row_count * width, transcendentals=0
        ),
    )(places, *pieces, weight, current, first, second, wanted)


def flipped(place, bits):
    bit = 1
    while bit <= bits:
        if bits & bit:
            place = place + bit * (1 - 2 * lax.rem(place // bit, 2))
        bit *= 2
    return place


PARTS = 4
AHEAD = 4


def exchange_kernel(
    replicas, codes, scales, outer, momentum, updates, got_codes, got_scales, pair_out, pair_in, own, update,
    code_send, code_recv, scale_send, scale_recv, pair_send, pair_recv,
    along_send, along_recv, across_send, across_recv, keep,
):
    groups = replicas // 2
    me = lax.axis_index("replica")
    group, side = me // 2, lax.rem(me, 2)
    partner = 2 * group + 1 - side
    fragment, width = outer.shape
    wide = width // PARTS

    barrier = pltpu.get_barrier_semaphore()
    pl.semaphore_signal(barrier, inc=1, device_id={"replica": partner}, device_id_type=MESH)
    for turn in range(1, groups):
        pl.semaphore_signal(
            barrier, inc=1, device_id={"replica": 2 * flipped(group, turn) + side}, device_id_type=MESH
        )
    pl.semaphore_wait(barrier, groups)

    order = [(turn, part) for part in range(PARTS) for turn in range(groups - 1, -1, -1)]

    def code_copy(i):
        turn, part = order[i]
        columns = pl.ds(part * wide, wide)
        return pltpu.make_async_remote_copy(
            src_ref=codes.at[2 * flipped(group, turn) + 1 - side, :, columns],
            dst_ref=got_codes.at[turn, :, columns],
            send_sem=code_send.at[i],
            recv_sem=code_recv.at[i],
            device_id={"replica": partner},
            device_id_type=MESH,
        )

    def scale_copy(turn):
        return pltpu.make_async_remote_copy(
            src_ref=scales.at[2 * flipped(group, turn) + 1 - side],
            dst_ref=got_scales.at[turn],
            send_sem=scale_send.at[turn],
            recv_sem=scale_recv.at[turn],
            device_id={"replica": partner},
            device_id_type=MESH,
        )

    def pair_copy(i):
        turn, part = order[i]
        columns = pl.ds(part * wide, wide)
        return pltpu.make_async_remote_copy(
            src_ref=pair_out.at[turn - 1, :, columns],
            dst_ref=pair_in.at[turn - 1, :, columns],
            send_sem=pair_send.at[i],
            recv_sem=pair_recv.at[i],
            device_id={"replica": 2 * flipped(group, turn) + side},
            device_id_type=MESH,
        )

    for turn in range(groups):
        scale_copy(turn).start()
    for i in range(AHEAD):
        code_copy(i).start()
    def add_pair(i):
        turn, part = order[i]
        if part == 0:
            scale_copy(turn).wait()
        code_copy(i).wait()
        if i + AHEAD < len(order):
            code_copy(i + AHEAD).start()
        mine = 2 * flipped(group, turn) + side

        def body(step, carry):
            rows = pl.ds(pl.multiple_of(step * TILE, TILE), TILE)
            my_scales = scales[mine, rows, :].astype(jnp.float32)
            their_scales = got_scales[turn, rows, :].astype(jnp.float32)
            for block in range(wide // BLOCK):
                at = part * (wide // BLOCK) + block
                columns = slice(at * BLOCK, (at + 1) * BLOCK)
                total = (
                    codes[mine, rows, columns].astype(jnp.float32) * my_scales[:, at : at + 1]
                    + got_codes[turn, rows, columns].astype(jnp.float32) * their_scales[:, at : at + 1]
                )
                if turn:
                    pair_out[turn - 1, rows, columns] = total.astype(jnp.bfloat16)
                else:
                    own[rows, columns] = total
            return carry

        lax.fori_loop(0, fragment // TILE, body, 0)
        if turn:
            pair_copy(i).start()

    hops = []
    bit = groups // 2
    while bit:
        hops += [(bit, held) for held in range(0, groups, 2 * bit)]
        bit //= 2

    def place_of(held, part):
        return updates.at[2 * flipped(group, held) + side, :, pl.ds(part * wide, wide)]

    def source_of(held, part):
        return update.at[:, pl.ds(part * wide, wide)] if held == 0 else place_of(held, part)

    def along_copy(hop, part):
        bit, held = hops[hop]
        return pltpu.make_async_remote_copy(
            src_ref=source_of(held, part),
            dst_ref=place_of(held, part),
            send_sem=along_send.at[hop * PARTS + part],
            recv_sem=along_recv.at[hop * PARTS + part],
            device_id={"replica": 2 * flipped(group, bit) + side},
            device_id_type=MESH,
        )

    def across_copy(held, part):
        return pltpu.make_async_remote_copy(
            src_ref=source_of(held, part),
            dst_ref=place_of(held, part),
            send_sem=across_send.at[held * PARTS + part],
            recv_sem=across_recv.at[held * PARTS + part],
            device_id={"replica": partner},
            device_id_type=MESH,
        )

    def send_on(held, part):
        for hop, (bit, taken) in enumerate(hops):
            if taken == held:
                along_copy(hop, part).start()
        across_copy(held, part).start()

    def finish_part(part):
        for i, (turn, which) in enumerate(order):
            if turn and which == part:
                pair_copy(i).wait()

        def finish(step, carry):
            rows = pl.ds(pl.multiple_of(step * TILE, TILE), TILE)
            for start in range(part * wide, (part + 1) * wide, 2 * BLOCK):
                columns = slice(start, start + 2 * BLOCK)
                total = own[rows, columns]
                for turn in range(1, groups):
                    total = total + pair_in[turn - 1, rows, columns].astype(jnp.float32)
                average = total * (1.0 / replicas)
                moved = outer_mu * outer[rows, columns] + average
                momentum[rows, columns] = moved
                update[rows, columns] = (average + outer_mu * moved).astype(jnp.bfloat16)
            return carry

        lax.fori_loop(0, fragment // TILE, finish, 0)
        send_on(0, part)

    def pass_on(part):
        for hop, (bit, held) in enumerate(hops):
            along_copy(hop, part).wait_recv()
            send_on(held + bit, part)

    for part in range(PARTS + 2):
        if part < PARTS:
            for i in range(part * groups, (part + 1) * groups):
                add_pair(i)
        if 0 < part <= PARTS:
            finish_part(part - 1)
        if part > 1:
            pass_on(part - 2)
    own_copy = pltpu.make_async_copy(update, updates.at[me], keep)
    own_copy.start()
    own_copy.wait()
    for part in range(PARTS):
        for hop in range(len(hops)):
            along_copy(hop, part).wait_send()
        for held in range(groups):
            across_copy(held, part).wait()


def exchange(codes, scales, outer_momentum, replicas):
    fragment, width = outer_momentum.shape
    groups = replicas // 2
    dma = pltpu.SemaphoreType.DMA
    vmem = pl.BlockSpec(memory_space=pltpu.VMEM)
    return pl.pallas_call(
        functools.partial(exchange_kernel, replicas),
        out_shape=(
            jax.ShapeDtypeStruct((fragment, width), jnp.float32),
            jax.ShapeDtypeStruct((replicas, fragment, width), jnp.bfloat16),
        ),
        in_specs=[vmem] * 3,
        out_specs=(vmem, pl.BlockSpec(memory_space=pl.ANY)),
        scratch_shapes=[
            pltpu.VMEM((groups, fragment, width), jnp.bfloat16),
            pltpu.VMEM((groups, fragment, BLOCK), jnp.bfloat16),
            pltpu.VMEM((groups - 1, fragment, width), jnp.bfloat16),
            pltpu.VMEM((groups - 1, fragment, width), jnp.bfloat16),
            pltpu.VMEM((fragment, width), jnp.float32),
            pltpu.VMEM((fragment, width), jnp.bfloat16),
            dma((groups * PARTS,)),
            dma((groups * PARTS,)),
            dma((groups,)),
            dma((groups,)),
            dma((groups * PARTS,)),
            dma((groups * PARTS,)),
            dma(((groups - 1) * PARTS,)),
            dma(((groups - 1) * PARTS,)),
            dma((groups * PARTS,)),
            dma((groups * PARTS,)),
            dma,
        ],
        compiler_params=pltpu.CompilerParams(
            collective_id=0, has_side_effects=True, vmem_limit_bytes=40 * 2**20
        ),
    )(codes.reshape(replicas, fragment, width), scales.reshape(replicas, fragment, BLOCK), outer_momentum)


def outer_kernel(weight, update, new_weight):
    new_weight[...] = weight[...] - outer_rate * update[0].astype(jnp.float32)


def outer_step(weight, updates):
    replicas, fragment, width = updates.shape
    rows = pl.BlockSpec((fragment, width), lambda step: (step, 0))
    return pl.pallas_call(
        outer_kernel,
        grid=(replicas,),
        out_shape=jax.ShapeDtypeStruct(weight.shape, jnp.float32),
        in_specs=[rows, pl.BlockSpec((1, fragment, width), lambda step: (step, 0, 0))],
        out_specs=rows,
        compiler_params=pltpu.CompilerParams(vmem_limit_bytes=32 * 2**20),
    )(weight, updates)


def shards(weight, first_moment, second_moment, outer_momentum, act_table, token_ids, targets):
    row_count, width = weight.shape
    replicas = lax.axis_size("replica")
    fragment = row_count // replicas
    whole_tiles = fragment % TILE == 0 and width % (2 * BLOCK * PARTS) == 0 and width // BLOCK <= BLOCK
    devices = lax.axis_size("mp")
    if not whole_tiles or replicas < 4 or replicas & (replicas - 1) or devices & (devices - 1):
        return shards_plain(
            weight, first_moment, second_moment, outer_momentum, act_table, token_ids, targets
        )
    wanted = jnp.swapaxes(targets[0], 1, 2)
    order, bit = [0], devices // 2
    inputs = [[jnp.take(act_table, token_ids[0, step], axis=0, mode="clip")] for step in range(STEPS)]
    while bit:
        to_other = [(device, device ^ bit) for device in range(devices)]
        order += [held + bit for held in order]
        inputs = [pieces + [lax.ppermute(piece, "mp", to_other) for piece in pieces] for pieces in inputs]
        bit //= 2
    places = lax.axis_index("mp") ^ jnp.array(order, jnp.int32)
    current, first, second = first_step(
        places, inputs[0], weight, first_moment[0], second_moment[0], wanted[0]
    )
    codes, scales = second_step(places, inputs[1], weight, current, first, second, wanted[1])
    momentum, updates = exchange(codes, scales, outer_momentum, replicas)
    return (outer_step(weight, updates), momentum)


def solution(mesh):
    in_specs = (
        P("mp", None),
        P("replica", "mp", None),
        P("replica", "mp", None),
        P(("mp", "replica"), None),
        P(None, "mp"),
        P("replica", None, None),
        P("replica", None, None, "mp"),
    )
    out_specs = (P("mp", None), P(("mp", "replica"), None))
    return jax.shard_map(shards, mesh=mesh, in_specs=in_specs, out_specs=out_specs, check_vma=False)
```
